128 devices in a mesh: ex: 16 (over y, z_lo, core), lg: 8 (over x, z_hi).
Axes of the slice: x: 4, y: 4, z: 4 (z_hi: 2, z_lo: 2; z = z_hi * 2 + z_lo), core: 2. Of those that a mesh axis runs over, the one named last changes fastest.
Arguments:
- query_factors: bfloat16 [32, 16, 32, 128, 128], P(None, 'ex', 'lg'), may hold values from -6 to 6
- rewards: float32 [32, 16], replicated, may hold values from -4 to 4
- ranking: int32 [32, 16], replicated, may hold values from 0 to 15, each once within a row
- list_len: int32 [32], replicated, may hold values from 1 to 16
- store_slab: bfloat16 [4096, 32, 4096], P('ex', 'lg')
Outputs:
- scores: float32 [32, 4096], P('lg', 'ex')
The draws below stay inside these ranges and needn't reach their ends.
Inputs may be any that keep to these rules, and one draw needn't show every extreme that they name: Each row of ranking names every response of its list once.
All inputs are finite; a program needn't handle non-finite values.
Results may differ from the reference program's by a relative error of at most 0.0029.
Values may be sent and summed in bfloat16 or wider, within the bound.
No kernel may reach another device: no remote copies, remote signals or barrier semaphores. Data moves between devices by JAX's collectives and lax.ppermute only.
A program may use at most 64 MiB of HBM per device.

```python
import math
import jax
import jax.numpy as jnp
from jax import lax

Q = 32
K = 16
R = 64
RT = 128
NS_DEV = 256
F = 4096
LAYERS = 32
NS = 4096
N_EX = 16


def draw_list_len(key, part):
    first_key, second_key, third_key = jax.random.split(key, 3)
    base = jax.random.randint(first_key, (Q,), 1, K + 1)
    longest = jax.random.randint(second_key, (), 0, Q)
    shortest = (longest + 1 + jax.random.randint(third_key, (), 0, Q - 1)) % Q
    places = jnp.arange(Q)
    return jnp.where(places == longest, K, jnp.where(places == shortest, 1, base)).astype(jnp.int32)


def draw_store_slab(key, part):
    first_key, second_key = jax.random.split(key, 2)
    layer = jnp.arange(LAYERS, dtype=jnp.float32) / max(LAYERS - 1, 1)
    row_scale = jnp.exp(jax.random.uniform(second_key, (NS, 1, 1), jnp.float32, 0.0, math.log(10.0)))
    layer_scale = 3.0 ** layer
    base = jax.random.normal(first_key, (NS, LAYERS, F), jnp.float32)
    return (base * layer_scale[None, :, None] * row_scale).astype(jnp.bfloat16)


def steps_of(stream_key, dims, cuts, least, largest):
    def one(axis_at, parts):
        steps = jax.random.uniform(jax.random.fold_in(jax.random.fold_in(stream_key, 6), axis_at), (parts,), jnp.float32, least / len(cuts), largest / len(cuts))
        return jnp.repeat(jnp.exp(steps), dims[axis_at] // parts).reshape((-1,) + (1,) * (len(dims) - axis_at - 1))

    loudness = one(*cuts[0])
    for cut in cuts[1:]:
        loudness = loudness * one(*cut)
    return loudness


def bell_draw(own_key, extent, width, most, cuts=(), kind=jnp.bfloat16):
    values = jax.random.normal(own_key, extent, jnp.float32) * width
    if len(cuts) > 0:
        values = steps_of(own_key, extent, cuts, -0.22, 0.18) * values
    return jnp.clip(values, min=-most, max=most).astype(kind)


def setup_inputs(seed: int = 0) -> dict:
    arg_keys = jax.random.split(jax.random.key(seed), 6)
    query_factors = bell_draw(arg_keys[0], (Q, K, LAYERS, RT, 2 * R), 1.0, 6.0, ((1, 16), (2, 8)))
    rewards = bell_draw(arg_keys[1], (Q, K), 1.0, 4.0, (), jnp.float32)
    ranking = jax.vmap(lambda own: jax.random.permutation(own, K))(jax.random.split(arg_keys[2], Q)).reshape((Q, K)).astype(jnp.int32)
    list_len = draw_list_len(jax.random.fold_in(arg_keys[5], 71), 0)
    store_slab = draw_store_slab(jax.random.fold_in(arg_keys[5], 71), 0)
    return {"query_factors": query_factors, "rewards": rewards, "ranking": ranking, "list_len": list_len, "store_slab": store_slab}


EPS = 1e-06

def list_weights(rewards, ranking, list_len):
    count = rewards.shape[1]
    ordered = jnp.take_along_axis(rewards, ranking, axis=1)
    expo = jnp.exp(ordered)
    tail = jnp.cumsum(expo[:, ::-1], axis=1)[:, ::-1]
    place = jnp.arange(count, dtype=jnp.int32)[None, :]
    active = (place < list_len[:, None]).astype(jnp.float32)
    lead = jnp.cumsum(active / tail, axis=1)
    sorted_w = expo * lead - active
    match = (ranking[:, :, None] == jnp.arange(count, dtype=jnp.int32)[None, None, :]).astype(jnp.float32)
    return lax.optimization_barrier(jnp.sum(sorted_w[:, :, None] * match, axis=1))

def reference(query_factors, rewards, ranking, list_len, store_slab):
    weights = list_weights(rewards, ranking, list_len)

    def one_query(pair):
        facs, wrow = pair
        values = facs.astype(jnp.float32)
        grads = jnp.einsum('kltb,klta->klba', values[..., R:], values[..., :R], precision=lax.Precision.HIGHEST)
        grads = grads * RT ** (-0.5)
        weighted = wrow[:, None, None, None] * grads
        return lax.optimization_barrier(jnp.sum(weighted, axis=0))
    qgrad = lax.map(one_query, (query_factors, weights)).reshape(Q, LAYERS * R * R).astype(jnp.bfloat16)
    qfloat = qgrad.astype(jnp.float32)
    blocks = store_slab.reshape(N_EX, NS_DEV, LAYERS * R * R)

    def one_block(block):
        values = block.astype(jnp.float32)
        norm_sq = lax.optimization_barrier(jnp.sum(values * values, axis=1))
        raw = jnp.dot(qfloat, values.T, precision=lax.Precision.HIGHEST)
        return raw * lax.rsqrt(norm_sq + EPS)[None, :]
    scores = lax.map(one_block, blocks)
    return jnp.transpose(scores, (1, 0, 2)).reshape(Q, N_EX * NS_DEV)
```

```python
import jax
import jax.numpy as jnp
from jax import lax
from jax.experimental import pallas as pl
from jax.experimental.pallas import tpu as pltpu
from jax.sharding import PartitionSpec as P

EPS = 1e-06
F32 = jnp.float32
BF16 = jnp.bfloat16
HIGH = lax.Precision.HIGHEST
VMEM = 24 << 20
Q_STEP = 8


def params():
    return pltpu.CompilerParams(vmem_limit_bytes=VMEM)


def whole(shape):
    return pl.BlockSpec(shape, lambda *_: (0,) * len(shape))


def my_weights(rew, rank, length, me):
    count = rew.shape[0]
    ordered = jnp.zeros_like(rew)
    for k in range(count):
        ordered = ordered + jnp.where(rank == k, rew[k : k + 1, :], 0.0)
    expo = jnp.exp(ordered)
    rows = [expo[j : j + 1, :] for j in range(count)]
    tails = [None] * count
    total = None
    for j in reversed(range(count)):
        total = rows[j] if total is None else total + rows[j]
        tails[j] = total
    lead = None
    out = jnp.zeros_like(rows[0])
    for j in range(count):
        active = (length > j).astype(F32)
        term = active / tails[j]
        lead = term if lead is None else lead + term
        out = out + jnp.where(rank[j : j + 1, :] == me, rows[j] * lead - active, 0.0)
    return out


def outer_kernel(x_ref, rew_ref, rank_ref, len_ref, mine_ref, other_ref, w_ref, m_ref):
    queries = rew_ref.shape[1]
    layers = x_ref.shape[1]
    tokens = x_ref.shape[2]
    half = x_ref.shape[3] // 2
    lanes = 2 * half
    step_rows = layers * Q_STEP
    ex = lax.axis_index("ex")
    core = lax.rem(ex, 2)
    step = pl.program_id(0)

    @pl.when(step == 0)
    def _():
        w = my_weights(rew_ref[...], rank_ref[...], len_ref[...], ex) * tokens ** (-0.5)
        at = lax.broadcasted_iota(jnp.int32, (queries, queries), 0)
        to = lax.broadcasted_iota(jnp.int32, (queries, queries), 1)
        column = jnp.sum(jnp.where(at == to, w, 0.0), axis=1, keepdims=True)
        w_ref[...] = jnp.broadcast_to(column, w_ref.shape)

    for q in range(Q_STEP):
        w = w_ref[pl.ds(step * Q_STEP + q, 1), :]
        for layer in range(layers):
            x = x_ref[q, layer]
            inp = x[:, :half]
            twice = jnp.concatenate([inp, inp], axis=1)
            m = lax.dot_general(
                x[:, half:], twice, (((0,), (0,)), ((), ())), preferred_element_type=F32
            )
            m_ref[pl.ds(layer * Q_STEP + q, half, stride=step_rows), :] = m * w
    low = lax.broadcasted_iota(jnp.int32, (step_rows, lanes), 1) < half
    for which, ref in ((core, mine_ref), (1 - core, other_ref)):
        for piece in range(ref.shape[0]):
            for t in range(2):
                row = (which * (half // 2) + 4 * piece + 2 * t) * step_rows
                even = m_ref[pl.ds(pl.multiple_of(row, step_rows), step_rows), :]
                odd = m_ref[pl.ds(pl.multiple_of(row + step_rows, step_rows), step_rows), :]
                both = jnp.where(low, even, odd).reshape(layers, Q_STEP, lanes)
                ref[piece, :, :, t * lanes : (t + 1) * lanes] = both


def outer(factors, rew, rank, length, chips):
    queries, layers, tokens, lanes = factors.shape
    half = lanes // 2
    part = (chips, layers, queries, 2 * lanes)
    block = (chips, layers, Q_STEP, 2 * lanes)
    return pl.pallas_call(
        outer_kernel,
        grid=(queries // Q_STEP,),
        in_specs=[
            pl.BlockSpec((Q_STEP, layers, tokens, lanes), lambda i: (i, 0, 0, 0)),
            whole(rew.shape),
            whole(rank.shape),
            whole(length.shape),
        ],
        out_specs=[pl.BlockSpec(block, lambda i: (0, 0, i, 0))] * 2,
        out_shape=[jax.ShapeDtypeStruct(part, F32)] * 2,
        scratch_shapes=[
            pltpu.VMEM((queries, lanes), F32),
            pltpu.VMEM((half * layers * Q_STEP, lanes), F32),
        ],
        compiler_params=params(),
        name="outer",
    )(factors, rew, rank, length)


def pair_kernel(mine_ref, got_ref, send_ref, own_ref):
    chip = lax.div(lax.axis_index("ex"), 2)
    for s in range(mine_ref.shape[0]):
        send_ref[s] = (mine_ref[s] + got_ref[s]).astype(BF16)
    own_ref[...] = mine_ref[chip] + got_ref[chip]


def pair(mine, got):
    return pl.pallas_call(
        pair_kernel,
        in_specs=[whole(mine.shape)] * 2,
        out_specs=[whole(mine.shape), whole(mine.shape[1:])],
        grid=(1,),
        out_shape=[
            jax.ShapeDtypeStruct(mine.shape, BF16),
            jax.ShapeDtypeStruct(mine.shape[1:], F32),
        ],
        compiler_params=params(),
        name="pair",
    )(mine, got)


def total_kernel(own_ref, got_ref, out_ref):
    chip = lax.div(lax.axis_index("ex"), 2)
    total = own_ref[...]
    for s in range(got_ref.shape[0]):
        total = total + jnp.where(chip == s, 0.0, got_ref[s].astype(F32))
    total = total.astype(BF16)
    for s in range(out_ref.shape[0]):
        out_ref[s] = total


def total(own, got):
    return pl.pallas_call(
        total_kernel,
        in_specs=[whole(own.shape), whole(got.shape)],
        out_specs=whole(got.shape),
        grid=(1,),
        out_shape=jax.ShapeDtypeStruct(got.shape, BF16),
        compiler_params=params(),
        name="total",
    )(own, got)


def relay_kernel(x_ref, s_ref, n_ref):
    rows, layers, width = x_ref.shape
    depth = s_ref.shape[2]
    v = x_ref[...].reshape(rows * layers, width)
    for g in range(width // depth):
        s_ref[g] = v[:, g * depth : (g + 1) * depth]
    f = v.astype(F32)
    acc = None
    for c in range(width // 128):
        t = f[:, c * 128 : (c + 1) * 128]
        acc = t * t if acc is None else acc + t * t
    acc = jnp.sum(acc.reshape(rows, layers, 128), axis=1)
    n_ref[...] = lax.dot_general(
        jnp.ones((8, 128), F32),
        acc,
        (((1,), (1,)), ((), ())),
        precision=HIGH,
        preferred_element_type=F32,
    )


def relay(store, depth, block=128):
    rows, layers, width = store.shape
    parts = width // depth
    return pl.pallas_call(
        relay_kernel,
        grid=(rows // block,),
        in_specs=[pl.BlockSpec((block, layers, width), lambda i: (i, 0, 0))],
        out_specs=[
            pl.BlockSpec((parts, block * layers, depth), lambda i: (0, i, 0)),
            pl.BlockSpec((8, block), lambda i: (0, i)),
        ],
        out_shape=[
            jax.ShapeDtypeStruct((parts, rows * layers, depth), BF16),
            jax.ShapeDtypeStruct((8, rows), F32),
        ],
        compiler_params=params(),
        cost_estimate=pl.CostEstimate(flops=64 << 20, bytes_accessed=40 << 20, transcendentals=0),
        name="relay",
    )(store)


def score_kernel(s_ref, own_ref, got_ref, n_ref, out_ref, g_ref):
    layers = own_ref.shape[1]
    queries = own_ref.shape[2]
    rows = s_ref.shape[1] // layers
    chips = own_ref.shape[0]
    core = lax.rem(lax.axis_index("ex"), 2)
    step = pl.program_id(0)

    @pl.when(step == 0)
    def _():
        g_ref[...] = jnp.zeros_like(g_ref)

    def add(ref, piece):
        q = ref[piece].reshape(layers * queries, ref.shape[3])
        g_ref[...] += lax.dot_general(
            s_ref[0], q, (((1,), (1,)), ((), ())), preferred_element_type=F32
        )

    piece = lax.rem(step, chips)
    own = lax.div(step, chips) == core

    @pl.when(own)
    def _():
        add(own_ref, piece)

    @pl.when(jnp.logical_not(own))
    def _():
        add(got_ref, piece)

    @pl.when(step == pl.num_programs(0) - 1)
    def _():
        g = g_ref[...]
        at = lax.rem(lax.broadcasted_iota(jnp.int32, g.shape, 0), layers)
        to = lax.div(lax.broadcasted_iota(jnp.int32, g.shape, 1), queries)
        g = jnp.where(at == to, g, 0.0)
        g = jnp.sum(g.reshape(rows, layers, layers * queries), axis=1)
        row = lax.broadcasted_iota(jnp.int32, (queries, layers * queries), 0)
        col = lax.rem(lax.broadcasted_iota(jnp.int32, (queries, layers * queries), 1), queries)
        pick = jnp.where(row == col, 1.0, 0.0).astype(F32)
        scores = lax.dot_general(
            pick, g, (((1,), (1,)), ((), ())), precision=HIGH, preferred_element_type=F32
        )
        each = queries // out_ref.shape[0]
        for j in range(out_ref.shape[0]):
            out_ref[j, :each, :] = scores[j * each : (j + 1) * each, :]
            out_ref[j, each:, :] = n_ref[: 8 - each, :]


def score(packed, own, got, norms, groups):
    parts, rows, depth = packed.shape
    layers, queries = own.shape[1:3]
    return pl.pallas_call(
        score_kernel,
        grid=(parts,),
        in_specs=[
            pl.BlockSpec((1, rows, depth), lambda i: (i, 0, 0)),
            whole(own.shape),
            whole(got.shape),
            whole(norms.shape),
        ],
        out_specs=whole((groups, 8, rows // layers)),
        out_shape=jax.ShapeDtypeStruct((groups, 8, rows // layers), F32),
        scratch_shapes=[pltpu.VMEM((rows, layers * queries), F32)],
        compiler_params=params(),
        name="score",
    )(packed, own, got, norms)


def last_kernel(got_ref, out_ref):
    each = out_ref.shape[0]
    total = got_ref[0]
    for s in range(1, got_ref.shape[0]):
        total = total + got_ref[s]
    out_ref[...] = total[:each, :] * lax.rsqrt(total[each : each + 1, :] + EPS)


def last(got, each):
    return pl.pallas_call(
        last_kernel,
        in_specs=[whole(got.shape)],
        out_specs=whole((each, got.shape[2])),
        grid=(1,),
        out_shape=jax.ShapeDtypeStruct((each, got.shape[2]), F32),
        compiler_params=params(),
        name="last",
    )(got)


def solution(mesh):
    ex, lg = mesh.shape["ex"], mesh.shape["lg"]
    chips = ex // 2
    same_core = [[2 * i + c for i in range(chips)] for c in range(2)]
    twin = [(i, i ^ 1) for i in range(ex)]

    def per_device(query_factors, rewards, ranking, list_len, store_slab):
        queries, _, layers, tokens, lanes = query_factors.shape
        factors = query_factors.reshape(queries, layers, tokens, lanes)
        mine, other = outer(factors, rewards.T, ranking.T, list_len[None, :], chips)
        got = lax.ppermute(other, "ex", twin)
        send, own = pair(mine, got)
        packed, norms = relay(store_slab, 2 * lanes)
        got = lax.all_to_all(send, "ex", 0, 0, axis_index_groups=same_core)
        summed = total(own, got)
        held = lax.all_to_all(summed, "ex", 0, 0, axis_index_groups=same_core)
        got = lax.ppermute(held, "ex", twin)
        partial = score(packed, held, got, norms, lg)
        got = lax.all_to_all(partial, "lg", 0, 0)
        return last(got, queries // lg)

    placed = (P(None, "ex", "lg", None, None), P(), P(), P(), P("ex", "lg", None))
    return jax.shard_map(
        per_device, mesh=mesh, in_specs=placed, out_specs=P("lg", "ex"), check_vma=False
    )
```
